32 devices in a mesh: grp: 2 (over x), node: 8 (over z, y), tm: 2 (over core).
Axes of the slice: x: 2, y: 2, z: 4, core: 2. Of those that a mesh axis runs over, the one named last changes fastest.
Arguments:
- scaled_kelvin: float32 [128, 8192], P(('grp', 'node', 'tm')), parts along dimension 0, may hold values from 0.5 to 1.5
- surface_emittance: float32 [16384], P('grp'), parts along dimension 0, may hold values from 0.2 to 1
- loss_factors: float32 [128, 8192], P(('grp', 'node', 'tm')), parts along dimension 0, may hold values from -6 to 6
- gebhart_tiles: bfloat16 [128, 32, 128, 128], P(('grp', 'node')), parts along dimension 0, may hold values from 1.4603138e-06 to 0.0014648438
- tile_target_index: int32 [128, 32], P(('grp', 'node')), parts along dimension 0, may hold values from 0 to 63
- tile_slots_occupied: int32 [128], P(('grp', 'node')), parts along dimension 0, may hold values from 16 to 32, as said below
Outputs:
- temp_sensitivity: float32 [128, 8192], P(('grp', 'node', 'tm')), parts along dimension 0
The draws below stay inside these ranges and needn't reach their ends.
There are 2 independent parts, one for each index of `grp`. The reference program is written for one: setup_inputs(seed, part) draws one part's arguments, and reference() takes and returns one part's arrays. A program takes and returns all parts, laid end to end along the dimension named above; each array names one. Nothing has to cross between parts.
Inputs may be any that keep to these rules, and one draw needn't show every extreme that they name: A row's slots k below tile_slots_occupied are used, the others are ignored; some row of every variant uses all 32.
All inputs are finite; a program needn't handle non-finite values.
Results may differ from the reference program's by a relative error of at most 0.0036.
Values may be sent and summed in bfloat16 or wider, within the bound.
A program may use at most 192 MiB of HBM per device.

```python
import math
import jax
import jax.numpy as jnp
from jax import lax

BLOCK = 128
SLOTS = 32
NBLOCKS = 64
SURFACE_COUNT = 8192
EPOCH_COUNT = 64


def draw_tile_slots_occupied(key, part):
    key_base = jax.random.fold_in(key, 11)
    key_forced = jax.random.fold_in(key, 13)
    counted = jax.random.randint(key_base, (NBLOCKS,), SLOTS // 2, SLOTS + 1)
    forced = jax.random.randint(key_forced, (), 0, NBLOCKS)
    counted = jnp.where(jnp.arange(NBLOCKS) == forced, SLOTS, counted)
    return counted.astype(jnp.int32)


def with_ends(entries, own_key, low, high):
    spot = [jax.random.randint(jax.random.fold_in(own_key, axis), (), 0, length) for axis, length in enumerate(entries.shape)]
    main_axis = entries.shape.index(max(entries.shape))
    next_to = spot[:main_axis] + [(spot[main_axis] + 1) % entries.shape[main_axis]] + spot[main_axis + 1:]
    return entries.at[tuple(spot)].set(low).at[tuple(next_to)].set(high)


def block_levels(rng, extent, pieces, low, top_value):
    factor_of, own = 1.0, jax.random.fold_in(rng, 6)
    for dim, shards_of in pieces:
        heights = jnp.exp(jax.random.uniform(jax.random.fold_in(own, dim), (shards_of,), jnp.float32, low / len(pieces), top_value / len(pieces)))
        factor_of = factor_of * jnp.repeat(heights, extent[dim] // shards_of).reshape([-1 if axis == dim else 1 for axis in range(len(extent))])
    return factor_of


def scatter_about(rng, dims, spread, reach, pieces=(), kind=jnp.bfloat16):
    factor_of = block_levels(rng, dims, pieces, -0.22, 0.18) if pieces else 1.0
    array = jax.random.normal(rng, dims, jnp.float32) * spread * factor_of
    return jnp.minimum(jnp.maximum(array, -reach), reach).astype(kind)


def setup_inputs(seed: int = 0, part: int = 0) -> dict:
    seeds = jax.random.split(jax.random.key(seed), 7)
    own_keys = jax.random.split(jax.random.fold_in(seeds[6], part), 7)
    scaled_kelvin = jnp.clip(0.5 + 1.0 * jax.random.uniform(own_keys[0], (EPOCH_COUNT, SURFACE_COUNT), jnp.float32) ** block_levels(own_keys[0], (EPOCH_COUNT, SURFACE_COUNT), ((0, 16),), -0.2, 0.2), 0.5, 1.5)
    surface_emittance = jnp.clip(jax.random.uniform(own_keys[1], (SURFACE_COUNT,), jnp.float32, 0.2, 1.0), 0.2, 1.0)
    loss_factors = scatter_about(own_keys[2], (EPOCH_COUNT, SURFACE_COUNT), 1.0, 6.0, ((0, 16),), jnp.float32)
    gebhart_tiles = jnp.clip(jnp.exp(math.log(0.0014648438) - 6.9108525 * jax.random.uniform(own_keys[3], (NBLOCKS, SLOTS, BLOCK, BLOCK), jnp.float32) ** block_levels(own_keys[3], (NBLOCKS, SLOTS, BLOCK, BLOCK), ((0, 8),), -0.2, 0.2)), 1.4603137969970703e-06, 0.0014648438).astype(jnp.bfloat16)
    tile_target_index = with_ends(jax.random.randint(own_keys[4], (NBLOCKS, SLOTS), 0, NBLOCKS), jax.random.fold_in(own_keys[4], 1), 0, NBLOCKS - 1).astype(jnp.int32)
    tile_slots_occupied = draw_tile_slots_occupied(jax.random.fold_in(jax.random.fold_in(seeds[6], part), 71), part)
    return {"scaled_kelvin": scaled_kelvin, "surface_emittance": surface_emittance, "loss_factors": loss_factors, "gebhart_tiles": gebhart_tiles, "tile_target_index": tile_target_index, "tile_slots_occupied": tile_slots_occupied}


def reference(scaled_kelvin, surface_emittance, loss_factors, gebhart_tiles, tile_target_index, tile_slots_occupied):
    radiant_output = (surface_emittance[None, :] * scaled_kelvin ** 4).astype(jnp.bfloat16)
    emit_wide = radiant_output.astype(jnp.float32)
    epoch_range = scaled_kelvin.shape[0]
    panel_view = emit_wide.reshape(epoch_range, NBLOCKS, BLOCK)
    in_use = jnp.arange(SLOTS, dtype=jnp.int32)[None, :] < tile_slots_occupied[:, None]

    def row_flux(operands):
        tiles, columns, usable = operands
        picked = jnp.take(panel_view, columns, axis=1) * usable.astype(jnp.float32)[None, :, None]
        return jnp.einsum("tkj,kij->ti", picked, tiles.astype(jnp.float32))

    flux = lax.map(row_flux, (gebhart_tiles, tile_target_index, in_use))
    flux = flux.transpose(1, 0, 2).reshape(epoch_range, SURFACE_COUNT)
    weight = loss_factors * (flux - emit_wide)
    rounded = lax.optimization_barrier(weight.astype(jnp.bfloat16)).astype(jnp.float32)
    weight_rows = rounded.reshape(epoch_range, NBLOCKS, BLOCK).transpose(1, 0, 2)

    def add_row(collected, operands):
        tiles, columns, usable, weight_row = operands
        contrib = jnp.einsum("ti,kij->tkj", weight_row, tiles.astype(jnp.float32))
        targets = jnp.where(usable, columns, NBLOCKS)
        return collected.at[:, targets, :].add(contrib, mode="drop"), None

    start_sum = jnp.zeros((epoch_range, NBLOCKS, BLOCK), jnp.float32)
    collected, unused = lax.scan(add_row, start_sum, (gebhart_tiles, tile_target_index, in_use, weight_rows))
    costate_vector = collected.reshape(epoch_range, SURFACE_COUNT) - weight
    return 4.0 * surface_emittance[None, :] * scaled_kelvin ** 3 * costate_vector
```

```python
import functools

import jax
import jax.numpy as jnp
from jax import lax
from jax.experimental import pallas as pl
from jax.experimental.pallas import tpu as pltpu
from jax.sharding import PartitionSpec as P

MESH = pl.DeviceIdType.MESH
F32 = jnp.float32
BF16 = jnp.bfloat16
CHUNK = 16


def kernel(
    n,
    kelvin_ref,
    emit_ref,
    loss_ref,
    tiles_hbm,
    gather_ref,
    prev_ref,
    last_ref,
    out_ref,
    tiles,
    em_recv,
    em,
    loss_send,
    loss_recv,
    loss_rows,
    neg_weight,
    running,
    mix,
    stage,
    adj_recv,
    tile_sem,
    em_send_sem,
    em_recv_sem,
    loss_send_sem,
    loss_recv_sem,
    adj_send_sem,
    adj_recv_sem,
):
    me = lax.axis_index("node")
    rows, slots, side = tiles.shape[0], tiles.shape[1], tiles.shape[2]
    blocks = emit_ref.shape[0]
    tl = kelvin_ref.shape[0]
    samples = tl * n
    chunks = blocks // CHUNK
    ch_rows = CHUNK * tl
    entries = rows * slots

    def tile_copy(r):
        return pltpu.make_async_copy(tiles_hbm.at[r], tiles.at[r], tile_sem.at[r])

    for r in range(rows):
        tile_copy(r).start()

    barrier = pltpu.get_barrier_semaphore()
    for o in range(1, n):
        pl.semaphore_signal(
            barrier, inc=1, device_id={"node": lax.rem(me + o, n)}, device_id_type=MESH
        )

    def emit_chunk(ch, carry):
        first = pl.multiple_of(ch * ch_rows, ch_rows)
        for i in range(CHUNK):
            cols = pl.ds(pl.multiple_of((ch * CHUNK + i) * side, side), side)
            t2 = kelvin_ref[:, cols] * kelvin_ref[:, cols]
            stage[i * tl : (i + 1) * tl, :] = emit_ref[pl.ds(ch * CHUNK + i, 1), :] * (t2 * t2)
        em_recv[me, pl.ds(first, ch_rows), :] = stage[...].astype(BF16)
        for i in range(CHUNK):
            cols = pl.ds(pl.multiple_of((ch * CHUNK + i) * side, side), side)
            stage[i * tl : (i + 1) * tl, :] = loss_ref[:, cols]
        loss_send[pl.ds(first, ch_rows), :] = stage[...].astype(BF16)
        return carry

    lax.fori_loop(0, chunks, emit_chunk, 0)
    pl.semaphore_wait(barrier, n - 1)

    def em_copy(o, src, dst):
        return pltpu.make_async_remote_copy(
            src_ref=em_recv.at[src],
            dst_ref=em_recv.at[src],
            send_sem=em_send_sem.at[o],
            recv_sem=em_recv_sem.at[o],
            device_id={"node": dst},
            device_id_type=MESH,
        )

    def loss_copy(o, src, dst):
        part = pl.multiple_of(dst * (rows * tl), rows * tl)
        return pltpu.make_async_remote_copy(
            src_ref=loss_send.at[pl.ds(part, rows * tl)],
            dst_ref=loss_recv.at[src],
            send_sem=loss_send_sem.at[o],
            recv_sem=loss_recv_sem.at[o],
            device_id={"node": dst},
            device_id_type=MESH,
        )

    for o in range(1, n):
        em_copy(o, me, lax.rem(me + o, n)).start()
    for o in range(1, n):
        loss_copy(o, me, lax.rem(me + o, n)).start()

    em[blocks] = jnp.zeros((samples, side), BF16)
    neg_weight[rows] = jnp.zeros((samples, side), F32)
    running[entries] = jnp.zeros((samples, side), F32)
    own_part = pl.multiple_of(me * (rows * tl), rows * tl)
    loss_recv[me] = loss_send[pl.ds(own_part, rows * tl), :]

    for o in range(1, n):
        em_copy(o, lax.rem(me + n - o, n), lax.rem(me + o, n)).wait()

    def em_chunk(ch, carry):
        first = pl.multiple_of(ch * ch_rows, ch_rows)
        for s in range(n):
            mix[pl.ds(s, ch_rows, stride=n), :] = em_recv[s, pl.ds(first, ch_rows), :].astype(F32)
        for i in range(CHUNK):
            em[ch * CHUNK + i] = mix[i * samples : (i + 1) * samples, :].astype(BF16)
        return carry

    lax.fori_loop(0, chunks, em_chunk, 0)

    for o in range(1, n):
        loss_copy(o, lax.rem(me + n - o, n), lax.rem(me + o, n)).wait()
    for s in range(n):
        loss_rows[pl.ds(s, rows * tl, stride=n), :] = loss_recv[s].astype(F32)
    for r in range(rows):
        tile_copy(r).wait()

    def row_step(r, carry):
        flux = jnp.zeros((samples, side), F32)
        for k in range(slots):
            flux += lax.dot_general(
                em[gather_ref[r * slots + k]],
                tiles[r, k],
                (((1,), (1,)), ((), ())),
                preferred_element_type=F32,
            )
        own = em[me * rows + r].astype(F32)
        here = loss_rows[pl.ds(pl.multiple_of(r * samples, samples), samples), :]
        weight = here * (flux - own)
        neg_weight[r] = -weight
        weight_b = weight.astype(BF16)
        for k in range(slots):
            contrib = jnp.dot(weight_b, tiles[r, k], preferred_element_type=F32)
            running[r * slots + k] = contrib + running[prev_ref[r * slots + k]]
        return carry

    lax.fori_loop(0, rows, row_step, 0)

    def adj_copy(o, ch, src, dst):
        first = pl.multiple_of(ch * ch_rows, ch_rows)
        return pltpu.make_async_remote_copy(
            src_ref=em_recv.at[dst, pl.ds(first, ch_rows)],
            dst_ref=adj_recv.at[src, pl.ds(first, ch_rows)],
            send_sem=adj_send_sem.at[o, ch],
            recv_sem=adj_recv_sem.at[o, ch],
            device_id={"node": dst},
            device_id_type=MESH,
        )

    def send_chunk(ch, carry):
        first = pl.multiple_of(ch * ch_rows, ch_rows)
        for i in range(CHUNK):
            c = ch * CHUNK + i
            off = c - me * rows
            mine = jnp.where((off >= 0) & (off < rows), off, rows)
            mix[i * samples : (i + 1) * samples, :] = running[last_ref[c]] + neg_weight[mine]
        for s in range(n):
            em_recv[s, pl.ds(first, ch_rows), :] = mix[pl.ds(s, ch_rows, stride=n), :].astype(BF16)
        for o in range(1, n):
            adj_copy(o, ch, me, lax.rem(me + o, n)).start()
        return carry

    lax.fori_loop(0, chunks, send_chunk, 0)

    def sum_chunk(ch, carry):
        first = pl.multiple_of(ch * ch_rows, ch_rows)
        total = em_recv[me, pl.ds(first, ch_rows), :].astype(F32)
        for o in range(1, n):
            src = lax.rem(me + n - o, n)
            adj_copy(o, ch, src, lax.rem(me + o, n)).wait()
            total += adj_recv[src, pl.ds(first, ch_rows), :].astype(F32)
        stage[...] = total
        for i in range(CHUNK):
            cols = pl.ds(pl.multiple_of((ch * CHUNK + i) * side, side), side)
            out_ref[:, cols] = stage[i * tl : (i + 1) * tl, :]
        return carry

    lax.fori_loop(0, chunks, sum_chunk, 0)


def on_device(
    n,
    scaled_kelvin,
    surface_emittance,
    loss_factors,
    gebhart_tiles,
    tile_target_index,
    tile_slots_occupied,
):
    rows, slots, side = gebhart_tiles.shape[:3]
    tl, surfaces = scaled_kelvin.shape
    blocks = surfaces // side
    samples = tl * n
    entries = rows * slots

    in_use = jnp.arange(slots, dtype=jnp.int32)[None, :] < tile_slots_occupied[:, None]
    target = jnp.where(in_use, tile_target_index, blocks).reshape(entries)
    at = jnp.arange(entries, dtype=jnp.int32)
    same = (target[:, None] == target[None, :]) & (at[None, :] < at[:, None])
    prev = jnp.max(jnp.where(same, at[None, :], -1), axis=1)
    prev = jnp.where(prev < 0, entries, prev)
    hit = jnp.arange(blocks, dtype=jnp.int32)[:, None] == target[None, :]
    last = jnp.max(jnp.where(hit, at[None, :], -1), axis=1)
    last = jnp.where(last < 0, entries, last)

    vmem = pl.BlockSpec(memory_space=pltpu.VMEM)
    smem = pl.BlockSpec(memory_space=pltpu.SMEM)
    adjoint = pl.pallas_call(
        functools.partial(kernel, n),
        out_shape=jax.ShapeDtypeStruct((tl, surfaces), F32),
        in_specs=[vmem, vmem, vmem, pl.BlockSpec(memory_space=pl.ANY), smem, smem, smem],
        out_specs=vmem,
        scratch_shapes=[
            pltpu.VMEM(gebhart_tiles.shape, BF16),
            pltpu.VMEM((n, blocks * tl, side), BF16),
            pltpu.VMEM((blocks + 1, samples, side), BF16),
            pltpu.VMEM((blocks * tl, side), BF16),
            pltpu.VMEM((n, rows * tl, side), BF16),
            pltpu.VMEM((rows * samples, side), F32),
            pltpu.VMEM((rows + 1, samples, side), F32),
            pltpu.VMEM((entries + 1, samples, side), F32),
            pltpu.VMEM((CHUNK * samples, side), F32),
            pltpu.VMEM((CHUNK * tl, side), F32),
            pltpu.VMEM((n, blocks * tl, side), BF16),
            pltpu.SemaphoreType.DMA((rows,)),
            pltpu.SemaphoreType.DMA((n,)),
            pltpu.SemaphoreType.DMA((n,)),
            pltpu.SemaphoreType.DMA((n,)),
            pltpu.SemaphoreType.DMA((n,)),
            pltpu.SemaphoreType.DMA((n, blocks // CHUNK)),
            pltpu.SemaphoreType.DMA((n, blocks // CHUNK)),
        ],
        compiler_params=pltpu.CompilerParams(
            collective_id=0, has_side_effects=True, vmem_limit_bytes=60 * 2**20
        ),
    )(
        scaled_kelvin,
        surface_emittance.reshape(blocks, side),
        loss_factors,
        gebhart_tiles,
        target,
        prev,
        last,
    )
    return 4.0 * surface_emittance[None, :] * scaled_kelvin**3 * adjoint


def solution(mesh):
    placed = (
        P(("grp", "node", "tm"), None),
        P("grp"),
        P(("grp", "node", "tm"), None),
        P(("grp", "node"), None, None, None),
        P(("grp", "node"), None),
        P(("grp", "node")),
    )
    return jax.shard_map(
        functools.partial(on_device, mesh.shape["node"]),
        mesh=mesh,
        in_specs=placed,
        out_specs=P(("grp", "node", "tm"), None),
        check_vma=False,
    )
```

```python
import functools

import jax
import jax.numpy as jnp
from jax import lax
from jax.experimental import pallas as pl
from jax.experimental.pallas import tpu as pltpu
from jax.sharding import PartitionSpec as P

MESH = pl.DeviceIdType.MESH
F32 = jnp.float32
BF16 = jnp.bfloat16
CHUNK = 16


def kernel(
    n,
    kelvin_ref,
    emit_ref,
    loss_ref,
    tiles_hbm,
    gather_ref,
    prev_ref,
    last_ref,
    out_ref,
    tiles,
    em_recv,
    em,
    loss_send,
    loss_recv,
    loss_rows,
    neg_weight,
    running,
    mix,
    stage,
    keep,
    mid_recv,
    adj_recv,
    tile_sem,
    em_send_sem,
    em_recv_sem,
    loss_send_sem,
    loss_recv_sem,
    mid_send_sem,
    mid_recv_sem,
    adj_send_sem,
    adj_recv_sem,
):
    me = lax.axis_index("node")
    rows, slots, side = tiles.shape[0], tiles.shape[1], tiles.shape[2]
    blocks = emit_ref.shape[0]
    tl = kelvin_ref.shape[0]
    samples = tl * n
    chunks = blocks // CHUNK
    ch_rows = CHUNK * tl
    entries = rows * slots
    depth = n // 2
    line, y = me // 2, lax.rem(me, 2)
    partner = line * 2 + 1 - y

    def along(d):
        return lax.rem(line + d + depth, depth) * 2

    def tile_copy(r):
        return pltpu.make_async_copy(tiles_hbm.at[r], tiles.at[r], tile_sem.at[r])

    for r in range(rows):
        tile_copy(r).start()

    barrier = pltpu.get_barrier_semaphore()
    for o in range(1, n):
        pl.semaphore_signal(
            barrier, inc=1, device_id={"node": lax.rem(me + o, n)}, device_id_type=MESH
        )

    def emit_chunk(ch, carry):
        first = pl.multiple_of(ch * ch_rows, ch_rows)
        for i in range(CHUNK):
            cols = pl.ds(pl.multiple_of((ch * CHUNK + i) * side, side), side)
            t2 = kelvin_ref[:, cols] * kelvin_ref[:, cols]
            stage[i * tl : (i + 1) * tl, :] = emit_ref[pl.ds(ch * CHUNK + i, 1), :] * (t2 * t2)
        em_recv[me, ch] = stage[...].astype(BF16)
        for i in range(CHUNK):
            cols = pl.ds(pl.multiple_of((ch * CHUNK + i) * side, side), side)
            stage[i * tl : (i + 1) * tl, :] = loss_ref[:, cols]
        loss_send[pl.ds(first, ch_rows), :] = stage[...].astype(BF16)
        return carry

    lax.fori_loop(0, chunks, emit_chunk, 0)
    pl.semaphore_wait(barrier, n - 1)

    def em_copy(o, src, dst):
        return pltpu.make_async_remote_copy(
            src_ref=em_recv.at[src],
            dst_ref=em_recv.at[src],
            send_sem=em_send_sem.at[o],
            recv_sem=em_recv_sem.at[o],
            device_id={"node": dst},
            device_id_type=MESH,
        )

    def loss_copy(o, src, dst):
        part = pl.multiple_of(dst * (rows * tl), rows * tl)
        return pltpu.make_async_remote_copy(
            src_ref=loss_send.at[pl.ds(part, rows * tl)],
            dst_ref=loss_recv.at[src],
            send_sem=loss_send_sem.at[o],
            recv_sem=loss_recv_sem.at[o],
            device_id={"node": dst},
            device_id_type=MESH,
        )

    for d in reversed(range(1, depth)):
        em_copy(d, me, along(d) + y).start()
    em_copy(0, me, partner).start()
    for o in range(1, n):
        loss_copy(o, me, lax.rem(me + o, n)).start()

    em[blocks] = jnp.zeros((samples, side), BF16)
    neg_weight[rows] = jnp.zeros((samples, side), F32)
    running[entries] = jnp.zeros((samples, side), F32)
    own_part = pl.multiple_of(me * (rows * tl), rows * tl)
    loss_recv[me] = loss_send[pl.ds(own_part, rows * tl), :]

    for d in range(1, depth):
        em_copy(d, along(-d) + y, along(d) + y).wait()
        em_copy(depth + d, along(-d) + y, partner).start()
    em_copy(0, partner, partner).wait()
    for d in range(1, depth):
        em_copy(depth + d, along(-d) + 1 - y, partner).wait()

    def em_chunk(ch, carry):
        for s in range(n):
            mix[pl.ds(s, ch_rows, stride=n), :] = em_recv[s, ch].astype(F32)
        for i in range(CHUNK):
            em[ch * CHUNK + i] = mix[i * samples : (i + 1) * samples, :].astype(BF16)
        return carry

    lax.fori_loop(0, chunks, em_chunk, 0)

    for o in range(1, n):
        loss_copy(o, lax.rem(me + n - o, n), lax.rem(me + o, n)).wait()
    for s in range(n):
        loss_rows[pl.ds(s, rows * tl, stride=n), :] = loss_recv[s].astype(F32)
    for r in range(rows):
        tile_copy(r).wait()

    def row_step(r, carry):
        flux = jnp.zeros((samples, side), F32)
        for k in range(0, slots, 2):
            flux += lax.dot_general(
                jnp.concatenate(
                    [em[gather_ref[r * slots + k]], em[gather_ref[r * slots + k + 1]]], axis=1
                ),
                jnp.concatenate([tiles[r, k], tiles[r, k + 1]], axis=1),
                (((1,), (1,)), ((), ())),
                preferred_element_type=F32,
            )
        own = em[me * rows + r].astype(F32)
        here = loss_rows[pl.ds(pl.multiple_of(r * samples, samples), samples), :]
        weight = here * (flux - own)
        neg_weight[r] = -weight
        weight_b = weight.astype(BF16)
        for k in range(0, slots, 2):
            pair = jnp.concatenate([tiles[r, k], tiles[r, k + 1]], axis=1)
            contrib = jnp.dot(weight_b, pair, preferred_element_type=F32)
            for e in range(2):
                at = r * slots + k + e
                running[at] = contrib[:, e * side : (e + 1) * side] + running[prev_ref[at]]
        return carry

    lax.fori_loop(0, rows, row_step, 0)

    def mid_copy(ch):
        return pltpu.make_async_remote_copy(
            src_ref=em_recv.at[pl.ds(0, depth), ch],
            dst_ref=mid_recv.at[pl.ds(0, depth), ch],
            send_sem=mid_send_sem.at[ch],
            recv_sem=mid_recv_sem.at[ch],
            device_id={"node": partner},
            device_id_type=MESH,
        )

    def adj_copy(d, ch):
        return pltpu.make_async_remote_copy(
            src_ref=em_recv.at[depth + d, ch],
            dst_ref=adj_recv.at[d, ch],
            send_sem=adj_send_sem.at[d, ch],
            recv_sem=adj_recv_sem.at[d, ch],
            device_id={"node": along(d) + y},
            device_id_type=MESH,
        )

    def split_chunk(ch):
        for i in range(CHUNK):
            c = ch * CHUNK + i
            off = c - me * rows
            mine = jnp.where((off >= 0) & (off < rows), off, rows)
            mix[i * samples : (i + 1) * samples, :] = running[last_ref[c]] + neg_weight[mine]
        for z in range(depth):
            other = mix[pl.ds(2 * z + 1 - y, ch_rows, stride=n), :]
            em_recv[z, ch] = other.astype(BF16)
        mid_copy(ch).start()
        for z in range(depth):
            keep[z, ch] = mix[pl.ds(2 * z + y, ch_rows, stride=n), :]

    def pass_chunk(ch):
        mid_copy(ch).wait()
        for d in reversed(range(1, depth)):
            z = lax.rem(line + d, depth)
            em_recv[depth + d, ch] = (keep[z, ch] + mid_recv[z, ch].astype(F32)).astype(BF16)
            adj_copy(d, ch).start()

    split_chunk(0)

    def send_step(ch, carry):
        split_chunk(ch)
        pass_chunk(ch - 1)
        return carry

    lax.fori_loop(1, chunks, send_step, 0)
    pass_chunk(chunks - 1)

    def sum_chunk(ch, carry):
        total = keep[line, ch] + mid_recv[line, ch].astype(F32)
        for d in range(1, depth):
            adj_copy(d, ch).wait()
            total += adj_recv[d, ch].astype(F32)
        stage[...] = total
        for i in range(CHUNK):
            cols = pl.ds(pl.multiple_of((ch * CHUNK + i) * side, side), side)
            out_ref[:, cols] = stage[i * tl : (i + 1) * tl, :]
        return carry

    lax.fori_loop(0, chunks, sum_chunk, 0)


def on_device(
    n,
    scaled_kelvin,
    surface_emittance,
    loss_factors,
    gebhart_tiles,
    tile_target_index,
    tile_slots_occupied,
):
    rows, slots, side = gebhart_tiles.shape[:3]
    tl, surfaces = scaled_kelvin.shape
    blocks = surfaces // side
    samples = tl * n
    entries = rows * slots
    chunked = (blocks // CHUNK, CHUNK * tl, side)

    in_use = jnp.arange(slots, dtype=jnp.int32)[None, :] < tile_slots_occupied[:, None]
    target = jnp.where(in_use, tile_target_index, blocks).reshape(entries)
    at = jnp.arange(entries, dtype=jnp.int32)
    same = (target[:, None] == target[None, :]) & (at[None, :] < at[:, None])
    prev = jnp.max(jnp.where(same, at[None, :], -1), axis=1)
    prev = jnp.where(prev < 0, entries, prev)
    hit = jnp.arange(blocks, dtype=jnp.int32)[:, None] == target[None, :]
    last = jnp.max(jnp.where(hit, at[None, :], -1), axis=1)
    last = jnp.where(last < 0, entries, last)

    vmem = pl.BlockSpec(memory_space=pltpu.VMEM)
    smem = pl.BlockSpec(memory_space=pltpu.SMEM)
    adjoint = pl.pallas_call(
        functools.partial(kernel, n),
        out_shape=jax.ShapeDtypeStruct((tl, surfaces), F32),
        in_specs=[vmem, vmem, vmem, pl.BlockSpec(memory_space=pl.ANY), smem, smem, smem],
        out_specs=vmem,
        scratch_shapes=[
            pltpu.VMEM(gebhart_tiles.shape, BF16),
            pltpu.VMEM((n,) + chunked, BF16),
            pltpu.VMEM((blocks + 1, samples, side), BF16),
            pltpu.VMEM((blocks * tl, side), BF16),
            pltpu.VMEM((n, rows * tl, side), BF16),
            pltpu.VMEM((rows * samples, side), F32),
            pltpu.VMEM((rows + 1, samples, side), F32),
            pltpu.VMEM((entries + 1, samples, side), F32),
            pltpu.VMEM((CHUNK * samples, side), F32),
            pltpu.VMEM((CHUNK * tl, side), F32),
            pltpu.VMEM((n // 2,) + chunked, F32),
            pltpu.VMEM((n // 2,) + chunked, BF16),
            pltpu.VMEM((n // 2,) + chunked, BF16),
            pltpu.SemaphoreType.DMA((rows,)),
            pltpu.SemaphoreType.DMA((n,)),
            pltpu.SemaphoreType.DMA((n,)),
            pltpu.SemaphoreType.DMA((n,)),
            pltpu.SemaphoreType.DMA((n,)),
            pltpu.SemaphoreType.DMA((blocks // CHUNK,)),
            pltpu.SemaphoreType.DMA((blocks // CHUNK,)),
            pltpu.SemaphoreType.DMA((n // 2, blocks // CHUNK)),
            pltpu.SemaphoreType.DMA((n // 2, blocks // CHUNK)),
        ],
        compiler_params=pltpu.CompilerParams(
            collective_id=0, has_side_effects=True, vmem_limit_bytes=62 * 2**20
        ),
    )(
        scaled_kelvin,
        surface_emittance.reshape(blocks, side),
        loss_factors,
        gebhart_tiles,
        target,
        prev,
        last,
    )
    return 4.0 * surface_emittance[None, :] * scaled_kelvin**3 * adjoint


def solution(mesh):
    placed = (
        P(("grp", "node", "tm"), None),
        P("grp"),
        P(("grp", "node", "tm"), None),
        P(("grp", "node"), None, None, None),
        P(("grp", "node"), None),
        P(("grp", "node")),
    )
    return jax.shard_map(
        functools.partial(on_device, mesh.shape["node"]),
        mesh=mesh,
        in_specs=placed,
        out_specs=P(("grp", "node", "tm"), None),
        check_vma=False,
    )
```

```python
import functools

import jax
import jax.numpy as jnp
from jax import lax
from jax.experimental import pallas as pl
from jax.experimental.pallas import tpu as pltpu
from jax.sharding import PartitionSpec as P

MESH = pl.DeviceIdType.MESH
F32 = jnp.float32
BF16 = jnp.bfloat16
CHUNK = 16


def kernel(
    n,
    kelvin_ref,
    emit_ref,
    loss_ref,
    tiles_hbm,
    gather_ref,
    chain_ref,
    out_ref,
    tiles,
    em_recv,
    em,
    loss_send,
    loss_recv,
    loss_rows,
    neg_weight,
    weight_b,
    running,
    mix,
    stage,
    keep,
    mid_recv,
    adj_recv,
    tile_sem,
    em_send_sem,
    em_recv_sem,
    loss_send_sem,
    loss_recv_sem,
    mid_send_sem,
    mid_recv_sem,
    adj_send_sem,
    adj_recv_sem,
):
    me = lax.axis_index("node")
    rows, slots, side = tiles.shape[0], tiles.shape[1], tiles.shape[2]
    blocks = emit_ref.shape[0]
    tl = kelvin_ref.shape[0]
    samples = tl * n
    chunks = blocks // CHUNK
    ch_rows = CHUNK * tl
    entries = rows * slots
    depth = n // 2
    line, y = me // 2, lax.rem(me, 2)
    partner = line * 2 + 1 - y

    def along(d):
        return lax.rem(line + d + depth, depth) * 2

    def tile_copy(r):
        return pltpu.make_async_copy(tiles_hbm.at[r], tiles.at[r], tile_sem.at[r])

    for r in range(rows):
        tile_copy(r).start()

    barrier = pltpu.get_barrier_semaphore()
    for o in range(1, n):
        pl.semaphore_signal(
            barrier, inc=1, device_id={"node": lax.rem(me + o, n)}, device_id_type=MESH
        )

    def emit_chunk(ch):
        for i in range(CHUNK):
            cols = pl.ds(pl.multiple_of((ch * CHUNK + i) * side, side), side)
            t2 = kelvin_ref[:, cols] * kelvin_ref[:, cols]
            stage[i * tl : (i + 1) * tl, :] = emit_ref[pl.ds(ch * CHUNK + i, 1), :] * (t2 * t2)
        em_recv[me, ch] = stage[...].astype(BF16)

    def loss_chunk(ch, carry):
        for i in range(CHUNK):
            cols = pl.ds(pl.multiple_of((ch * CHUNK + i) * side, side), side)
            stage[i * tl : (i + 1) * tl, :] = loss_ref[:, cols]
        first = pl.multiple_of(ch * ch_rows, ch_rows)
        loss_send[pl.ds(first, ch_rows), :] = stage[...].astype(BF16)
        return carry

    def em_copy(o, ch, src, dst):
        return pltpu.make_async_remote_copy(
            src_ref=em_recv.at[src, ch],
            dst_ref=em_recv.at[src, ch],
            send_sem=em_send_sem.at[o, ch],
            recv_sem=em_recv_sem.at[o, ch],
            device_id={"node": dst},
            device_id_type=MESH,
        )

    def loss_copy(o, src, dst):
        part = pl.multiple_of(dst * (rows * tl), rows * tl)
        return pltpu.make_async_remote_copy(
            src_ref=loss_send.at[pl.ds(part, rows * tl)],
            dst_ref=loss_recv.at[src],
            send_sem=loss_send_sem.at[o],
            recv_sem=loss_recv_sem.at[o],
            device_id={"node": dst},
            device_id_type=MESH,
        )

    def em_start(ch):
        for d in reversed(range(1, depth)):
            em_copy(d, ch, me, along(d) + y).start()
        em_copy(0, ch, me, partner).start()

    emit_chunk(0)
    pl.semaphore_wait(barrier, n - 1)
    em_start(0)

    def emit_step(ch, carry):
        emit_chunk(ch)
        em_start(ch)
        return carry

    lax.fori_loop(1, chunks, emit_step, 0)
    lax.fori_loop(0, chunks, loss_chunk, 0)
    for o in range(1, n):
        loss_copy(o, me, lax.rem(me + o, n)).start()

    em[blocks] = jnp.zeros((samples, side), BF16)
    neg_weight[rows] = jnp.zeros((samples, side), F32)
    running[0] = jnp.zeros((samples, side), F32)
    own_part = pl.multiple_of(me * (rows * tl), rows * tl)
    loss_recv[me] = loss_send[pl.ds(own_part, rows * tl), :]

    def forward_chunk(ch):
        for d in range(1, depth):
            em_copy(d, ch, along(-d) + y, along(d) + y).wait()
            em_copy(depth + d, ch, along(-d) + y, partner).start()

    def em_chunk(ch):
        em_copy(0, ch, partner, partner).wait()
        for d in range(1, depth):
            em_copy(depth + d, ch, along(-d) + 1 - y, partner).wait()
        for s in range(n):
            mix[pl.ds(s, ch_rows, stride=n), :] = em_recv[s, ch].astype(F32)
        for i in range(CHUNK):
            em[ch * CHUNK + i] = mix[i * samples : (i + 1) * samples, :].astype(BF16)

    forward_chunk(0)

    def gather_step(ch, carry):
        forward_chunk(ch)
        em_chunk(ch - 1)
        return carry

    lax.fori_loop(1, chunks, gather_step, 0)
    em_chunk(chunks - 1)

    for o in range(1, n):
        loss_copy(o, lax.rem(me + n - o, n), lax.rem(me + o, n)).wait()
    for s in range(n):
        loss_rows[pl.ds(s, rows * tl, stride=n), :] = loss_recv[s].astype(F32)
    for r in range(rows):
        tile_copy(r).wait()

    def ahead(r):
        flux = jnp.zeros((samples, side), F32)
        for k in range(0, slots, 2):
            flux += lax.dot_general(
                jnp.concatenate(
                    [em[gather_ref[r * slots + k]], em[gather_ref[r * slots + k + 1]]], axis=1
                ),
                jnp.concatenate([tiles[r, k], tiles[r, k + 1]], axis=1),
                (((1,), (1,)), ((), ())),
                preferred_element_type=F32,
            )
        own = em[me * rows + r].astype(F32)
        here = loss_rows[pl.ds(pl.multiple_of(r * samples, samples), samples), :]
        weight = here * (flux - own)
        neg_weight[r] = -weight
        weight_b[r] = weight.astype(BF16)

    def back(r):
        for k in range(0, slots, 2):
            pair = jnp.concatenate([tiles[r, k], tiles[r, k + 1]], axis=1)
            contrib = jnp.dot(weight_b[r], pair, preferred_element_type=F32)
            for e in range(2):
                at = r * slots + k + e
                running[at + 1] = contrib[:, e * side : (e + 1) * side] + running[chain_ref[at]]

    ahead(0)

    def row_step(r, carry):
        back(r - 1)
        ahead(r)
        return carry

    lax.fori_loop(1, rows, row_step, 0)
    back(rows - 1)

    def mid_copy(ch):
        return pltpu.make_async_remote_copy(
            src_ref=em_recv.at[pl.ds(0, depth), ch],
            dst_ref=mid_recv.at[pl.ds(0, depth), ch],
            send_sem=mid_send_sem.at[ch],
            recv_sem=mid_recv_sem.at[ch],
            device_id={"node": partner},
            device_id_type=MESH,
        )

    def adj_copy(d, ch):
        return pltpu.make_async_remote_copy(
            src_ref=em_recv.at[depth + d, ch],
            dst_ref=adj_recv.at[d, ch],
            send_sem=adj_send_sem.at[d, ch],
            recv_sem=adj_recv_sem.at[d, ch],
            device_id={"node": along(d) + y},
            device_id_type=MESH,
        )

    def split_chunk(ch):
        for i in range(CHUNK):
            c = ch * CHUNK + i
            off = c - me * rows
            mine = jnp.where((off >= 0) & (off < rows), off, rows)
            mix[i * samples : (i + 1) * samples, :] = running[chain_ref[entries + c]] + neg_weight[mine]
        for z in range(depth):
            other = mix[pl.ds(2 * z + 1 - y, ch_rows, stride=n), :]
            em_recv[z, ch] = other.astype(BF16)
        mid_copy(ch).start()
        for z in range(depth):
            keep[z, ch] = mix[pl.ds(2 * z + y, ch_rows, stride=n), :]

    def pass_chunk(ch):
        mid_copy(ch).wait()
        for d in reversed(range(1, depth)):
            z = lax.rem(line + d, depth)
            em_recv[depth + d, ch] = (keep[z, ch] + mid_recv[z, ch].astype(F32)).astype(BF16)
            adj_copy(d, ch).start()

    split_chunk(0)

    def send_step(ch, carry):
        split_chunk(ch)
        pass_chunk(ch - 1)
        return carry

    lax.fori_loop(1, chunks, send_step, 0)
    pass_chunk(chunks - 1)

    def sum_chunk(ch, carry):
        total = keep[line, ch] + mid_recv[line, ch].astype(F32)
        for d in range(1, depth):
            adj_copy(d, ch).wait()
            total += adj_recv[d, ch].astype(F32)
        stage[...] = total
        for i in range(CHUNK):
            cols = pl.ds(pl.multiple_of((ch * CHUNK + i) * side, side), side)
            t1 = kelvin_ref[:, cols]
            scale = 4.0 * emit_ref[pl.ds(ch * CHUNK + i, 1), :] * (t1 * t1 * t1)
            out_ref[:, cols] = scale * stage[i * tl : (i + 1) * tl, :]
        return carry

    lax.fori_loop(0, chunks, sum_chunk, 0)


def on_device(
    n,
    scaled_kelvin,
    surface_emittance,
    loss_factors,
    gebhart_tiles,
    tile_target_index,
    tile_slots_occupied,
):
    rows, slots, side = gebhart_tiles.shape[:3]
    tl, surfaces = scaled_kelvin.shape
    blocks = surfaces // side
    samples = tl * n
    entries = rows * slots
    chunked = (blocks // CHUNK, CHUNK * tl, side)

    in_use = jnp.arange(slots, dtype=jnp.int32)[None, :] < tile_slots_occupied[:, None]
    target = jnp.where(in_use, tile_target_index, blocks).reshape(entries)
    at = jnp.arange(entries, dtype=jnp.int32)
    column = jnp.concatenate([target, jnp.arange(blocks, dtype=jnp.int32)])
    limit = jnp.minimum(jnp.arange(entries + blocks, dtype=jnp.int32), entries)
    same = (column[:, None] == target[None, :]) & (at[None, :] < limit[:, None])
    chain = jnp.max(jnp.where(same, at[None, :] + 1, 0), axis=1)

    vmem = pl.BlockSpec(memory_space=pltpu.VMEM)
    smem = pl.BlockSpec(memory_space=pltpu.SMEM)
    return pl.pallas_call(
        functools.partial(kernel, n),
        out_shape=jax.ShapeDtypeStruct((tl, surfaces), F32),
        in_specs=[vmem, vmem, vmem, pl.BlockSpec(memory_space=pl.ANY), smem, smem],
        out_specs=vmem,
        scratch_shapes=[
            pltpu.VMEM(gebhart_tiles.shape, BF16),
            pltpu.VMEM((n,) + chunked, BF16),
            pltpu.VMEM((blocks + 1, samples, side), BF16),
            pltpu.VMEM((blocks * tl, side), BF16),
            pltpu.VMEM((n, rows * tl, side), BF16),
            pltpu.VMEM((rows * samples, side), F32),
            pltpu.VMEM((rows + 1, samples, side), F32),
            pltpu.VMEM((rows, samples, side), BF16),
            pltpu.VMEM((entries + 1, samples, side), F32),
            pltpu.VMEM((CHUNK * samples, side), F32),
            pltpu.VMEM((CHUNK * tl, side), F32),
            pltpu.VMEM((n // 2,) + chunked, F32),
            pltpu.VMEM((n // 2,) + chunked, BF16),
            pltpu.VMEM((n // 2,) + chunked, BF16),
            pltpu.SemaphoreType.DMA((rows,)),
            pltpu.SemaphoreType.DMA((n, blocks // CHUNK)),
            pltpu.SemaphoreType.DMA((n, blocks // CHUNK)),
            pltpu.SemaphoreType.DMA((n,)),
            pltpu.SemaphoreType.DMA((n,)),
            pltpu.SemaphoreType.DMA((blocks // CHUNK,)),
            pltpu.SemaphoreType.DMA((blocks // CHUNK,)),
            pltpu.SemaphoreType.DMA((n // 2, blocks // CHUNK)),
            pltpu.SemaphoreType.DMA((n // 2, blocks // CHUNK)),
        ],
        compiler_params=pltpu.CompilerParams(
            collective_id=0, has_side_effects=True, vmem_limit_bytes=62 * 2**20
        ),
    )(
        scaled_kelvin,
        surface_emittance.reshape(blocks, side),
        loss_factors,
        gebhart_tiles,
        target,
        chain,
    )


def solution(mesh):
    placed = (
        P(("grp", "node", "tm"), None),
        P("grp"),
        P(("grp", "node", "tm"), None),
        P(("grp", "node"), None, None, None),
        P(("grp", "node"), None),
        P(("grp", "node")),
    )
    return jax.shard_map(
        functools.partial(on_device, mesh.shape["node"]),
        mesh=mesh,
        in_specs=placed,
        out_specs=P(("grp", "node", "tm"), None),
        check_vma=False,
    )
```

```python
import functools

import jax
import jax.numpy as jnp
from jax import lax
from jax.experimental import pallas as pl
from jax.experimental.pallas import tpu as pltpu
from jax.sharding import PartitionSpec as P

MESH = pl.DeviceIdType.MESH
F32 = jnp.float32
BF16 = jnp.bfloat16
LANES = 128
CHUNK = 16


def kernel(
    n,
    kelvin_ref,
    emit_ref,
    loss_ref,
    tiles_hbm,
    target_ref,
    target_vec_ref,
    used_ref,
    out_ref,
    tiles,
    em_recv,
    em,
    loss_send,
    loss_recv,
    loss_rows,
    neg_weight,
    weight_b,
    wide,
    prev_vec,
    last_vec,
    prev_ref,
    last_ref,
    running,
    mix,
    stage,
    keep,
    mid_recv,
    adj_recv,
    tile_sem,
    index_sem,
    em_send_sem,
    em_recv_sem,
    loss_send_sem,
    loss_recv_sem,
    mid_send_sem,
    mid_recv_sem,
    adj_send_sem,
    adj_recv_sem,
):
    me = lax.axis_index("node")
    rows, slots, side = tiles.shape[0], tiles.shape[1], tiles.shape[2]
    blocks = emit_ref.shape[0]
    tl = kelvin_ref.shape[0]
    samples = tl * n
    chunks = blocks // CHUNK
    ch_rows = CHUNK * tl
    entries = rows * slots
    depth = n // 2
    line, y = me // 2, lax.rem(me, 2)
    partner = line * 2 + 1 - y

    def along(d):
        return lax.rem(line + d + depth, depth) * 2

    def column(r, k):
        return jnp.where(k < used_ref[r], target_ref[r, k], blocks)

    def tile_copy(r):
        return pltpu.make_async_copy(tiles_hbm.at[r], tiles.at[r], tile_sem.at[r])

    for r in range(rows):
        tile_copy(r).start()

    barrier = pltpu.get_barrier_semaphore()
    for o in range(1, n):
        pl.semaphore_signal(
            barrier, inc=1, device_id={"node": lax.rem(me + o, n)}, device_id_type=MESH
        )

    def emit_chunk(ch):
        for i in range(CHUNK):
            cols = pl.ds(pl.multiple_of((ch * CHUNK + i) * side, side), side)
            t2 = kelvin_ref[:, cols] * kelvin_ref[:, cols]
            stage[i * tl : (i + 1) * tl, :] = emit_ref[pl.ds(ch * CHUNK + i, 1), :] * (t2 * t2)
        em_recv[me, ch] = stage[...].astype(BF16)

    def loss_chunk(ch, carry):
        for i in range(CHUNK):
            cols = pl.ds(pl.multiple_of((ch * CHUNK + i) * side, side), side)
            stage[i * tl : (i + 1) * tl, :] = loss_ref[:, cols]
        first = pl.multiple_of(ch * ch_rows, ch_rows)
        loss_send[pl.ds(first, ch_rows), :] = stage[...].astype(BF16)
        return carry

    def em_copy(o, ch, src, dst):
        return pltpu.make_async_remote_copy(
            src_ref=em_recv.at[src, ch],
            dst_ref=em_recv.at[src, ch],
            send_sem=em_send_sem.at[o, ch],
            recv_sem=em_recv_sem.at[o, ch],
            device_id={"node": dst},
            device_id_type=MESH,
        )

    def loss_copy(o, src, dst):
        part = pl.multiple_of(dst * (rows * tl), rows * tl)
        return pltpu.make_async_remote_copy(
            src_ref=loss_send.at[pl.ds(part, rows * tl)],
            dst_ref=loss_recv.at[src],
            send_sem=loss_send_sem.at[o],
            recv_sem=loss_recv_sem.at[o],
            device_id={"node": dst},
            device_id_type=MESH,
        )

    def em_start(ch):
        for d in reversed(range(1, depth)):
            em_copy(d, ch, me, along(d) + y).start()
        em_copy(0, ch, me, partner).start()

    emit_chunk(0)
    pl.semaphore_wait(barrier, n - 1)
    em_start(0)

    def emit_step(ch, carry):
        emit_chunk(ch)
        em_start(ch)
        return carry

    lax.fori_loop(1, chunks, emit_step, 0)
    lax.fori_loop(0, chunks, loss_chunk, 0)
    for o in range(1, n):
        loss_copy(o, me, lax.rem(me + o, n)).start()

    em[blocks] = jnp.zeros((samples, side), BF16)
    neg_weight[rows] = jnp.zeros((samples, side), F32)
    running[0] = jnp.zeros((samples, side), F32)
    own_part = pl.multiple_of(me * (rows * tl), rows * tl)
    loss_recv[me] = loss_send[pl.ds(own_part, rows * tl), :]

    lane = lax.broadcasted_iota(jnp.int32, wide.shape, 1)
    row = lax.broadcasted_iota(jnp.int32, wide.shape, 0)
    wide[...] = jnp.full(wide.shape, blocks, jnp.int32)
    wide[:, :slots] = target_vec_ref[...]
    used = jnp.zeros(wide.shape, jnp.int32)
    for r in range(rows):
        used = jnp.where(row == r, used_ref[r], used)
    columns = jnp.where(lane < used, wide[...], blocks)
    place = row * slots + lane
    spot = lax.broadcasted_iota(jnp.int32, last_vec.shape, 0) * LANES
    spot += lax.broadcasted_iota(jnp.int32, last_vec.shape, 1)

    def index_step(r, carry):
        prev, last = carry
        for k in range(slots):
            at = r * slots + k
            c = column(r, k)
            prev = jnp.where((columns == c) & (place > at), at + 1, prev)
            last = jnp.where(spot == c, at + 1, last)
        return prev, last

    none = (jnp.zeros(prev_vec.shape, jnp.int32), jnp.zeros(last_vec.shape, jnp.int32))
    prev_vec[...], last_vec[...] = lax.fori_loop(0, rows, index_step, none)
    index_copies = (
        pltpu.make_async_copy(prev_vec, prev_ref, index_sem.at[0]),
        pltpu.make_async_copy(last_vec, last_ref, index_sem.at[1]),
    )
    for copy in index_copies:
        copy.start()

    def forward_chunk(ch):
        for d in range(1, depth):
            em_copy(d, ch, along(-d) + y, along(d) + y).wait()
            em_copy(depth + d, ch, along(-d) + y, partner).start()

    def em_chunk(ch):
        em_copy(0, ch, partner, partner).wait()
        for d in range(1, depth):
            em_copy(depth + d, ch, along(-d) + 1 - y, partner).wait()
        for s in range(n):
            mix[pl.ds(s, ch_rows, stride=n), :] = em_recv[s, ch].astype(F32)
        for i in range(CHUNK):
            em[ch * CHUNK + i] = mix[i * samples : (i + 1) * samples, :].astype(BF16)

    forward_chunk(0)

    def gather_step(ch, carry):
        forward_chunk(ch)
        em_chunk(ch - 1)
        return carry

    lax.fori_loop(1, chunks, gather_step, 0)
    em_chunk(chunks - 1)

    for o in range(1, n):
        loss_copy(o, lax.rem(me + n - o, n), lax.rem(me + o, n)).wait()
    for s in range(n):
        loss_rows[pl.ds(s, rows * tl, stride=n), :] = loss_recv[s].astype(F32)
    for r in range(rows):
        tile_copy(r).wait()

    def ahead(r):
        flux = jnp.zeros((samples, side), F32)
        for k in range(0, slots, 2):
            flux += lax.dot_general(
                jnp.concatenate(
                    [em[column(r, k)], em[column(r, k + 1)]], axis=1
                ),
                jnp.concatenate([tiles[r, k], tiles[r, k + 1]], axis=1),
                (((1,), (1,)), ((), ())),
                preferred_element_type=F32,
            )
        own = em[me * rows + r].astype(F32)
        here = loss_rows[pl.ds(pl.multiple_of(r * samples, samples), samples), :]
        weight = here * (flux - own)
        neg_weight[r] = -weight
        weight_b[r] = weight.astype(BF16)

    def back(r):
        for k in range(0, slots, 2):
            pair = jnp.concatenate([tiles[r, k], tiles[r, k + 1]], axis=1)
            contrib = jnp.dot(weight_b[r], pair, preferred_element_type=F32)
            for e in range(2):
                at = r * slots + k + e
                running[at + 1] = contrib[:, e * side : (e + 1) * side] + running[prev_ref[r, k + e]]

    for copy in index_copies:
        copy.wait()
    ahead(0)

    def row_step(r, carry):
        back(r - 1)
        ahead(r)
        return carry

    lax.fori_loop(1, rows, row_step, 0)
    back(rows - 1)

    def mid_copy(ch):
        return pltpu.make_async_remote_copy(
            src_ref=em_recv.at[pl.ds(0, depth), ch],
            dst_ref=mid_recv.at[pl.ds(0, depth), ch],
            send_sem=mid_send_sem.at[ch],
            recv_sem=mid_recv_sem.at[ch],
            device_id={"node": partner},
            device_id_type=MESH,
        )

    def adj_copy(d, ch):
        return pltpu.make_async_remote_copy(
            src_ref=em_recv.at[depth + d, ch],
            dst_ref=adj_recv.at[d, ch],
            send_sem=adj_send_sem.at[d, ch],
            recv_sem=adj_recv_sem.at[d, ch],
            device_id={"node": along(d) + y},
            device_id_type=MESH,
        )

    def split_chunk(ch):
        for i in range(CHUNK):
            c = ch * CHUNK + i
            off = c - me * rows
            mine = jnp.where((off >= 0) & (off < rows), off, rows)
            mix[i * samples : (i + 1) * samples, :] = running[last_ref[c // LANES, lax.rem(c, LANES)]] + neg_weight[mine]
        for z in range(depth):
            other = mix[pl.ds(2 * z + 1 - y, ch_rows, stride=n), :]
            em_recv[z, ch] = other.astype(BF16)
        mid_copy(ch).start()
        for z in range(depth):
            keep[z, ch] = mix[pl.ds(2 * z + y, ch_rows, stride=n), :]

    def pass_chunk(ch):
        mid_copy(ch).wait()
        for d in reversed(range(1, depth)):
            z = lax.rem(line + d, depth)
            em_recv[depth + d, ch] = (keep[z, ch] + mid_recv[z, ch].astype(F32)).astype(BF16)
            adj_copy(d, ch).start()

    split_chunk(0)

    def send_step(ch, carry):
        split_chunk(ch)
        pass_chunk(ch - 1)
        return carry

    lax.fori_loop(1, chunks, send_step, 0)
    pass_chunk(chunks - 1)

    def sum_chunk(ch, carry):
        total = keep[line, ch] + mid_recv[line, ch].astype(F32)
        for d in range(1, depth):
            adj_copy(d, ch).wait()
            total += adj_recv[d, ch].astype(F32)
        stage[...] = total
        for i in range(CHUNK):
            cols = pl.ds(pl.multiple_of((ch * CHUNK + i) * side, side), side)
            t1 = kelvin_ref[:, cols]
            scale = 4.0 * emit_ref[pl.ds(ch * CHUNK + i, 1), :] * (t1 * t1 * t1)
            out_ref[:, cols] = scale * stage[i * tl : (i + 1) * tl, :]
        return carry

    lax.fori_loop(0, chunks, sum_chunk, 0)


def on_device(
    n,
    scaled_kelvin,
    surface_emittance,
    loss_factors,
    gebhart_tiles,
    tile_target_index,
    tile_slots_occupied,
):
    rows, slots, side = gebhart_tiles.shape[:3]
    tl, surfaces = scaled_kelvin.shape
    blocks = surfaces // side
    samples = tl * n
    entries = rows * slots
    chunked = (blocks // CHUNK, CHUNK * tl, side)

    vmem = pl.BlockSpec(memory_space=pltpu.VMEM)
    smem = pl.BlockSpec(memory_space=pltpu.SMEM)
    return pl.pallas_call(
        functools.partial(kernel, n),
        out_shape=jax.ShapeDtypeStruct((tl, surfaces), F32),
        in_specs=[vmem, vmem, vmem, pl.BlockSpec(memory_space=pl.ANY), smem, vmem, smem],
        out_specs=vmem,
        scratch_shapes=[
            pltpu.VMEM(gebhart_tiles.shape, BF16),
            pltpu.VMEM((n,) + chunked, BF16),
            pltpu.VMEM((blocks + 1, samples, side), BF16),
            pltpu.VMEM((blocks * tl, side), BF16),
            pltpu.VMEM((n, rows * tl, side), BF16),
            pltpu.VMEM((rows * samples, side), F32),
            pltpu.VMEM((rows + 1, samples, side), F32),
            pltpu.VMEM((rows, samples, side), BF16),
            pltpu.VMEM((rows, LANES), jnp.int32),
            pltpu.VMEM((rows, LANES), jnp.int32),
            pltpu.VMEM((8, LANES), jnp.int32),
            pltpu.SMEM((rows, LANES), jnp.int32),
            pltpu.SMEM((8, LANES), jnp.int32),
            pltpu.VMEM((entries + 1, samples, side), F32),
            pltpu.VMEM((CHUNK * samples, side), F32),
            pltpu.VMEM((CHUNK * tl, side), F32),
            pltpu.VMEM((n // 2,) + chunked, F32),
            pltpu.VMEM((n // 2,) + chunked, BF16),
            pltpu.VMEM((n // 2,) + chunked, BF16),
            pltpu.SemaphoreType.DMA((rows,)),
            pltpu.SemaphoreType.DMA((2,)),
            pltpu.SemaphoreType.DMA((n, blocks // CHUNK)),
            pltpu.SemaphoreType.DMA((n, blocks // CHUNK)),
            pltpu.SemaphoreType.DMA((n,)),
            pltpu.SemaphoreType.DMA((n,)),
            pltpu.SemaphoreType.DMA((blocks // CHUNK,)),
            pltpu.SemaphoreType.DMA((blocks // CHUNK,)),
            pltpu.SemaphoreType.DMA((n // 2, blocks // CHUNK)),
            pltpu.SemaphoreType.DMA((n // 2, blocks // CHUNK)),
        ],
        compiler_params=pltpu.CompilerParams(
            collective_id=0, has_side_effects=True, vmem_limit_bytes=62 * 2**20
        ),
    )(
        scaled_kelvin,
        surface_emittance.reshape(blocks, side),
        loss_factors,
        gebhart_tiles,
        tile_target_index,
        tile_target_index,
        tile_slots_occupied,
    )


def solution(mesh):
    placed = (
        P(("grp", "node", "tm"), None),
        P("grp"),
        P(("grp", "node", "tm"), None),
        P(("grp", "node"), None, None, None),
        P(("grp", "node"), None),
        P(("grp", "node")),
    )
    return jax.shard_map(
        functools.partial(on_device, mesh.shape["node"]),
        mesh=mesh,
        in_specs=placed,
        out_specs=P(("grp", "node", "tm"), None),
        check_vma=False,
    )
```

```python
import functools

import jax
import jax.numpy as jnp
from jax import lax
from jax.experimental import pallas as pl
from jax.experimental.pallas import tpu as pltpu
from jax.sharding import PartitionSpec as P

MESH = pl.DeviceIdType.MESH
F32 = jnp.float32
BF16 = jnp.bfloat16
LANES = 128
CHUNK = 16


def kernel(
    n,
    kelvin_ref,
    emit_ref,
    loss_ref,
    tiles_hbm,
    target_ref,
    target_vec_ref,
    used_ref,
    out_ref,
    tiles,
    em_recv,
    em,
    loss_send,
    loss_recv,
    loss_rows,
    neg_weight,
    weight_b,
    wide,
    prev_vec,
    last_vec,
    prev_ref,
    last_ref,
    running,
    mix,
    stage,
    keep,
    mid_recv,
    adj_recv,
    tile_sem,
    index_sem,
    em_send_sem,
    em_recv_sem,
    loss_send_sem,
    loss_recv_sem,
    mid_send_sem,
    mid_recv_sem,
    adj_send_sem,
    adj_recv_sem,
):
    me = lax.axis_index("node")
    rows, slots, side = tiles.shape[0], tiles.shape[1], tiles.shape[2]
    blocks = emit_ref.shape[0]
    tl = kelvin_ref.shape[0]
    samples = tl * n
    chunks = blocks // CHUNK
    ch_rows = CHUNK * tl
    entries = rows * slots
    depth = n // 2
    line, y = me // 2, lax.rem(me, 2)
    partner = line * 2 + 1 - y

    def along(d):
        return lax.rem(line + d + depth, depth) * 2

    def column(r, k):
        return jnp.where(k < used_ref[r], target_ref[r, k], blocks)

    def tile_copy(r):
        return pltpu.make_async_copy(tiles_hbm.at[r], tiles.at[r], tile_sem.at[r])

    for r in range(rows):
        tile_copy(r).start()

    barrier = pltpu.get_barrier_semaphore()
    for o in range(1, n):
        pl.semaphore_signal(
            barrier, inc=1, device_id={"node": lax.rem(me + o, n)}, device_id_type=MESH
        )

    def emit_chunk(ch):
        for i in range(CHUNK):
            cols = pl.ds(pl.multiple_of((ch * CHUNK + i) * side, side), side)
            t2 = kelvin_ref[:, cols] * kelvin_ref[:, cols]
            stage[i * tl : (i + 1) * tl, :] = emit_ref[pl.ds(ch * CHUNK + i, 1), :] * (t2 * t2)
        em_recv[me, ch] = stage[...].astype(BF16)

    def loss_chunk(ch, carry):
        for i in range(CHUNK):
            cols = pl.ds(pl.multiple_of((ch * CHUNK + i) * side, side), side)
            stage[i * tl : (i + 1) * tl, :] = loss_ref[:, cols]
        first = pl.multiple_of(ch * ch_rows, ch_rows)
        loss_send[pl.ds(first, ch_rows), :] = stage[...].astype(BF16)
        return carry

    def em_copy(o, ch, src, dst):
        return pltpu.make_async_remote_copy(
            src_ref=em_recv.at[src, ch],
            dst_ref=em_recv.at[src, ch],
            send_sem=em_send_sem.at[o, ch],
            recv_sem=em_recv_sem.at[o, ch],
            device_id={"node": dst},
            device_id_type=MESH,
        )

    def loss_copy(o, src, dst):
        part = pl.multiple_of(dst * (rows * tl), rows * tl)
        return pltpu.make_async_remote_copy(
            src_ref=loss_send.at[pl.ds(part, rows * tl)],
            dst_ref=loss_recv.at[src],
            send_sem=loss_send_sem.at[o],
            recv_sem=loss_recv_sem.at[o],
            device_id={"node": dst},
            device_id_type=MESH,
        )

    def em_start(ch):
        for d in reversed(range(1, depth)):
            em_copy(d, ch, me, along(d) + y).start()
        em_copy(0, ch, me, partner).start()

    emit_chunk(0)
    pl.semaphore_wait(barrier, n - 1)
    em_start(0)

    def emit_step(ch, carry):
        emit_chunk(ch)
        em_start(ch)
        return carry

    lax.fori_loop(1, chunks, emit_step, 0)
    lax.fori_loop(0, chunks, loss_chunk, 0)
    for o in range(1, n):
        loss_copy(o, me, lax.rem(me + o, n)).start()

    em[blocks] = jnp.zeros((samples, side), BF16)
    neg_weight[rows] = jnp.zeros((samples, side), F32)
    running[0] = jnp.zeros((samples, side), F32)
    own_part = pl.multiple_of(me * (rows * tl), rows * tl)
    loss_recv[me] = loss_send[pl.ds(own_part, rows * tl), :]

    lane = lax.broadcasted_iota(jnp.int32, wide.shape, 1)
    row = lax.broadcasted_iota(jnp.int32, wide.shape, 0)
    wide[...] = jnp.full(wide.shape, blocks, jnp.int32)
    wide[:, :slots] = target_vec_ref[...]
    used = jnp.zeros(wide.shape, jnp.int32)
    for r in range(rows):
        used = jnp.where(row == r, used_ref[r], used)
    columns = jnp.where(lane < used, wide[...], blocks)
    place = row * slots + lane
    spot = lax.broadcasted_iota(jnp.int32, last_vec.shape, 0) * LANES
    spot += lax.broadcasted_iota(jnp.int32, last_vec.shape, 1)

    def index_step(r, carry):
        prev, last = carry
        for k in range(slots):
            at = r * slots + k
            c = column(r, k)
            prev = jnp.where((columns == c) & (place > at), at + 1, prev)
            last = jnp.where(spot == c, at + 1, last)
        return prev, last

    none = (jnp.zeros(prev_vec.shape, jnp.int32), jnp.zeros(last_vec.shape, jnp.int32))
    prev_vec[...], last_vec[...] = lax.fori_loop(0, rows, index_step, none)
    index_copies = (
        pltpu.make_async_copy(prev_vec, prev_ref, index_sem.at[0]),
        pltpu.make_async_copy(last_vec, last_ref, index_sem.at[1]),
    )
    for copy in index_copies:
        copy.start()

    def forward_chunk(ch):
        for d in range(1, depth):
            em_copy(d, ch, along(-d) + y, along(d) + y).wait()
            em_copy(depth + d, ch, along(-d) + y, partner).start()

    def em_chunk(ch):
        em_copy(0, ch, partner, partner).wait()
        for d in range(1, depth):
            em_copy(depth + d, ch, along(-d) + 1 - y, partner).wait()
        for s in range(n):
            mix[pl.ds(s, ch_rows, stride=n), :] = em_recv[s, ch].astype(F32)
        for i in range(CHUNK):
            em[ch * CHUNK + i] = mix[i * samples : (i + 1) * samples, :].astype(BF16)

    forward_chunk(0)

    def gather_step(ch, carry):
        forward_chunk(ch)
        em_chunk(ch - 1)
        return carry

    lax.fori_loop(1, chunks, gather_step, 0)
    em_chunk(chunks - 1)

    for o in range(1, n):
        loss_copy(o, lax.rem(me + n - o, n), lax.rem(me + o, n)).wait()
    for s in range(n):
        loss_rows[pl.ds(s, rows * tl, stride=n), :] = loss_recv[s].astype(F32)
    for r in range(rows):
        tile_copy(r).wait()

    def ahead(r):
        turned = jnp.zeros((side, samples), F32)
        for k in range(0, slots, 2):
            turned += lax.dot_general(
                jnp.concatenate([tiles[r, k], tiles[r, k + 1]], axis=1),
                jnp.concatenate([em[column(r, k)], em[column(r, k + 1)]], axis=1),
                (((1,), (1,)), ((), ())),
                preferred_element_type=F32,
            )
        flux = turned.T
        own = em[me * rows + r].astype(F32)
        here = loss_rows[pl.ds(pl.multiple_of(r * samples, samples), samples), :]
        weight = here * (flux - own)
        neg_weight[r] = -weight
        weight_b[r] = weight.astype(BF16)

    def back(r):
        for k in range(0, slots, 2):
            pair = jnp.concatenate([tiles[r, k], tiles[r, k + 1]], axis=1)
            contrib = jnp.dot(weight_b[r], pair, preferred_element_type=F32)
            for e in range(2):
                at = r * slots + k + e
                running[at + 1] = contrib[:, e * side : (e + 1) * side] + running[prev_ref[r, k + e]]

    for copy in index_copies:
        copy.wait()
    ahead(0)

    def row_step(r, carry):
        back(r - 1)
        ahead(r)
        return carry

    lax.fori_loop(1, rows, row_step, 0)
    back(rows - 1)

    def mid_copy(ch):
        return pltpu.make_async_remote_copy(
            src_ref=em_recv.at[pl.ds(0, depth), ch],
            dst_ref=mid_recv.at[pl.ds(0, depth), ch],
            send_sem=mid_send_sem.at[ch],
            recv_sem=mid_recv_sem.at[ch],
            device_id={"node": partner},
            device_id_type=MESH,
        )

    def adj_copy(d, ch):
        return pltpu.make_async_remote_copy(
            src_ref=em_recv.at[depth + d, ch],
            dst_ref=adj_recv.at[d, ch],
            send_sem=adj_send_sem.at[d, ch],
            recv_sem=adj_recv_sem.at[d, ch],
            device_id={"node": along(d) + y},
            device_id_type=MESH,
        )

    def split_chunk(ch):
        for i in range(CHUNK):
            c = ch * CHUNK + i
            off = c - me * rows
            mine = jnp.where((off >= 0) & (off < rows), off, rows)
            mix[i * samples : (i + 1) * samples, :] = running[last_ref[c // LANES, lax.rem(c, LANES)]] + neg_weight[mine]
        for z in range(depth):
            other = mix[pl.ds(2 * z + 1 - y, ch_rows, stride=n), :]
            em_recv[z, ch] = other.astype(BF16)
        mid_copy(ch).start()
        for z in range(depth):
            keep[z, ch] = mix[pl.ds(2 * z + y, ch_rows, stride=n), :]

    def pass_chunk(ch):
        mid_copy(ch).wait()
        for d in reversed(range(1, depth)):
            z = lax.rem(line + d, depth)
            em_recv[depth + d, ch] = (keep[z, ch] + mid_recv[z, ch].astype(F32)).astype(BF16)
            adj_copy(d, ch).start()

    split_chunk(0)

    def send_step(ch, carry):
        split_chunk(ch)
        pass_chunk(ch - 1)
        return carry

    lax.fori_loop(1, chunks, send_step, 0)
    pass_chunk(chunks - 1)

    def sum_chunk(ch, carry):
        total = keep[line, ch] + mid_recv[line, ch].astype(F32)
        for d in range(1, depth):
            adj_copy(d, ch).wait()
            total += adj_recv[d, ch].astype(F32)
        stage[...] = total
        for i in range(CHUNK):
            cols = pl.ds(pl.multiple_of((ch * CHUNK + i) * side, side), side)
            t1 = kelvin_ref[:, cols]
            scale = 4.0 * emit_ref[pl.ds(ch * CHUNK + i, 1), :] * (t1 * t1 * t1)
            out_ref[:, cols] = scale * stage[i * tl : (i + 1) * tl, :]
        return carry

    lax.fori_loop(0, chunks, sum_chunk, 0)


def on_device(
    n,
    scaled_kelvin,
    surface_emittance,
    loss_factors,
    gebhart_tiles,
    tile_target_index,
    tile_slots_occupied,
):
    rows, slots, side = gebhart_tiles.shape[:3]
    tl, surfaces = scaled_kelvin.shape
    blocks = surfaces // side
    samples = tl * n
    entries = rows * slots
    chunked = (blocks // CHUNK, CHUNK * tl, side)

    vmem = pl.BlockSpec(memory_space=pltpu.VMEM)
    smem = pl.BlockSpec(memory_space=pltpu.SMEM)
    return pl.pallas_call(
        functools.partial(kernel, n),
        out_shape=pltpu.VMEM((tl, surfaces), F32),
        in_specs=[vmem, vmem, vmem, pl.BlockSpec(memory_space=pl.ANY), smem, vmem, smem],
        out_specs=vmem,
        scratch_shapes=[
            pltpu.VMEM(gebhart_tiles.shape, BF16),
            pltpu.VMEM((n,) + chunked, BF16),
            pltpu.VMEM((blocks + 1, samples, side), BF16),
            pltpu.VMEM((blocks * tl, side), BF16),
            pltpu.VMEM((n, rows * tl, side), BF16),
            pltpu.VMEM((rows * samples, side), F32),
            pltpu.VMEM((rows + 1, samples, side), F32),
            pltpu.VMEM((rows, samples, side), BF16),
            pltpu.VMEM((rows, LANES), jnp.int32),
            pltpu.VMEM((rows, LANES), jnp.int32),
            pltpu.VMEM((8, LANES), jnp.int32),
            pltpu.SMEM((rows, LANES), jnp.int32),
            pltpu.SMEM((8, LANES), jnp.int32),
            pltpu.VMEM((entries + 1, samples, side), F32),
            pltpu.VMEM((CHUNK * samples, side), F32),
            pltpu.VMEM((CHUNK * tl, side), F32),
            pltpu.VMEM((n // 2,) + chunked, F32),
            pltpu.VMEM((n // 2,) + chunked, BF16),
            pltpu.VMEM((n // 2,) + chunked, BF16),
            pltpu.SemaphoreType.DMA((rows,)),
            pltpu.SemaphoreType.DMA((2,)),
            pltpu.SemaphoreType.DMA((n, blocks // CHUNK)),
            pltpu.SemaphoreType.DMA((n, blocks // CHUNK)),
            pltpu.SemaphoreType.DMA((n,)),
            pltpu.SemaphoreType.DMA((n,)),
            pltpu.SemaphoreType.DMA((blocks // CHUNK,)),
            pltpu.SemaphoreType.DMA((blocks // CHUNK,)),
            pltpu.SemaphoreType.DMA((n // 2, blocks // CHUNK)),
            pltpu.SemaphoreType.DMA((n // 2, blocks // CHUNK)),
        ],
        compiler_params=pltpu.CompilerParams(
            collective_id=0, has_side_effects=True, vmem_limit_bytes=62 * 2**20
        ),
    )(
        scaled_kelvin,
        surface_emittance.reshape(blocks, side),
        loss_factors,
        gebhart_tiles,
        tile_target_index,
        tile_target_index,
        tile_slots_occupied,
    )


def solution(mesh):
    placed = (
        P(("grp", "node", "tm"), None),
        P("grp"),
        P(("grp", "node", "tm"), None),
        P(("grp", "node"), None, None, None),
        P(("grp", "node"), None),
        P(("grp", "node")),
    )
    return jax.shard_map(
        functools.partial(on_device, mesh.shape["node"]),
        mesh=mesh,
        in_specs=placed,
        out_specs=P(("grp", "node", "tm"), None),
        check_vma=False,
    )
```
